32 devices in a mesh: section: 8 (over z, core), tensor: 4 (over y, x).
Axes of the slice: x: 2, y: 2, z: 4, core: 2. Of those that a mesh axis runs over, the one named last changes fastest.
Arguments:
- value_half: bfloat16 [8, 1024, 8192], P('section', None, 'tensor'), may hold values from -0.125 to 0.125
- out_half: bfloat16 [8, 8192, 1024], P('section', 'tensor'), may hold values from -0.0625 to 0.0625
- saved: bfloat16 [8, 2, 128, 2048], P('section', None, None, 'tensor'), may hold values from -6 to 6
- first_grad: bfloat16 [8, 128, 2048], P('section', None, 'tensor'), may hold values from -6 to 6
- head_grad: bfloat16 [2, 128, 2048], P(None, None, 'tensor'), may hold values from -6 to 6
Outputs:
- sent_grad: bfloat16 [8, 128, 2048], P('section', None, 'tensor')
- value_grad: bfloat16 [8, 1024, 8192], P('section', None, 'tensor')
- out_grad: bfloat16 [8, 8192, 1024], P('section', 'tensor')
The draws below stay inside these ranges and needn't reach their ends.
All inputs are finite; a program needn't handle non-finite values.
Results may differ from the reference program's by a relative error of at most 0.012.
Values may be sent and summed in bfloat16 or wider, within the bound.
A program may use at most 192 MiB of HBM per device.

```python
import jax
import jax.numpy as jnp
from jax import lax

D = 2048
FF = 8192
TOK = 128
N_SECTION = 8
N_TENSOR = 4


def level_of(rng, extent, cuts, smallest, largest):
    gain = 1.0
    for dim, parts in cuts:
        steps = jax.random.uniform(jax.random.fold_in(jax.random.fold_in(rng, 6), dim), (parts,), jnp.float32, smallest / len(cuts), largest / len(cuts))
        gain = gain * jnp.repeat(jnp.exp(steps), extent[dim] // parts).reshape((-1,) + (1,) * (len(extent) - 1 - dim))
    return gain


def centred(key, dims, spread, bound, pieces=(), kind=jnp.bfloat16):
    drawn = spread * jax.random.normal(key, dims, jnp.float32)
    if pieces:
        drawn = drawn * level_of(key, dims, pieces, -0.22, 0.18)
    return jnp.clip(drawn, -bound, bound).astype(kind)


def setup_inputs(seed: int = 0) -> dict:
    key_list = jax.random.split(jax.random.key(seed), 6)
    value_half = centred(key_list[0], (N_SECTION, D // 2, FF), D ** -0.5, 0.125, ((0, 8), (2, 4)))
    out_half = centred(key_list[1], (N_SECTION, FF, D // 2), FF ** -0.5, 0.0625, ((0, 8), (1, 4)))
    saved = centred(key_list[2], (N_SECTION, 2, TOK, D), 1.0, 6.0, ((0, 8), (3, 4)))
    first_grad = centred(key_list[3], (N_SECTION, TOK, D), 1.0, 6.0, ((0, 8), (2, 4)))
    head_grad = centred(key_list[4], (2, TOK, D), 1.0, 6.0, ((2, 4),))
    return {"value_half": value_half, "out_half": out_half, "saved": saved, "first_grad": first_grad, "head_grad": head_grad}


def silu_parts(preact):
    sigmoid_val = jax.nn.sigmoid(preact)
    return preact * sigmoid_val, sigmoid_val * (1.0 + preact * (1.0 - sigmoid_val))


def layer_back(inputs, incoming, w_value, w_out):
    preact = jnp.dot(inputs, w_value, preferred_element_type=jnp.float32)
    activation, slope = silu_parts(preact)
    activation = activation.astype(jnp.bfloat16)
    backgrad = jnp.dot(incoming, w_out.T, preferred_element_type=jnp.float32)
    grad_pre = (backgrad * slope).astype(jnp.bfloat16)
    group_width = FF // N_TENSOR
    grouped_grad = grad_pre.astype(jnp.float32).reshape(TOK, N_TENSOR, group_width)
    grouped_value = w_value.astype(jnp.float32).reshape(D, N_TENSOR, group_width)
    partials = jnp.einsum("tsh,dsh->std", grouped_grad, grouped_value)
    rounded = lax.optimization_barrier(partials.astype(jnp.bfloat16))
    summed = jnp.sum(rounded.astype(jnp.float32), axis=0)
    passed = (incoming.astype(jnp.float32) + summed).astype(jnp.bfloat16)
    value_term = jnp.dot(inputs.T, grad_pre, preferred_element_type=jnp.float32)
    out_term = jnp.dot(activation.T, incoming, preferred_element_type=jnp.float32)
    return passed, value_term, out_term


def reference(value_half, out_half, saved, first_grad, head_grad):
    section_count = N_SECTION
    sections = section_count // 2
    half_rows = D // 2
    w_values = jnp.concatenate([value_half[:sections], value_half[sections:]], axis=1)
    w_outs = jnp.concatenate([out_half[:sections], out_half[sections:]], axis=2)
    positions = jnp.arange(section_count, dtype=jnp.int32)

    def first_pass(position):
        section = (position % sections).astype(jnp.int32)
        return layer_back(saved[position, 0], first_grad[position], w_values[section], w_outs[section])[0]

    passed_first = lax.map(first_pass, positions)
    shifted = jnp.concatenate([passed_first[1:], jnp.zeros_like(passed_first[:1])], axis=0)
    head_full = head_grad[(positions // sections).astype(jnp.int32)]
    at_end = (positions % sections) == sections - 1
    incoming = jnp.where(at_end[:, None, None], head_full, shifted)

    def one_section(section):
        w_value = w_values[section]
        w_out = w_outs[section]
        results = []
        for device in (section, sections + section):
            first = layer_back(saved[device, 0], first_grad[device], w_value, w_out)
            second = layer_back(saved[device, 1], incoming[device], w_value, w_out)
            value_total = (first[1] + second[1]).astype(jnp.bfloat16)
            out_total = (first[2] + second[2]).astype(jnp.bfloat16)
            results.append((value_total, out_total, second[0]))
        value_sum = (results[0][0].astype(jnp.float32) + results[1][0].astype(jnp.float32)).astype(jnp.bfloat16)
        out_sum = (results[0][1].astype(jnp.float32) + results[1][1].astype(jnp.float32)).astype(jnp.bfloat16)
        return value_sum, out_sum, results[0][2], results[1][2]

    value_sums, out_sums, down_sent, up_sent = lax.map(one_section, jnp.arange(sections, dtype=jnp.int32))
    value_grad = jnp.concatenate([value_sums[:, :half_rows], value_sums[:, half_rows:]], axis=0)
    out_grad = jnp.concatenate([out_sums[:, :, :half_rows], out_sums[:, :, half_rows:]], axis=0)
    sent_grad = jnp.concatenate([down_sent, up_sent], axis=0)
    return (sent_grad, value_grad, out_grad)
```

```python
import jax
import jax.numpy as jnp
from jax import lax
from jax.sharding import PartitionSpec as P

F32 = jnp.float32
BF16 = jnp.bfloat16


def dot(left, right, left_dim, right_dim):
    return lax.dot_general(
        left, right, (((left_dim,), (right_dim,)), ((), ())), preferred_element_type=F32
    )


def split_copies(gathered):
    half = gathered.shape[1] // 2
    return jnp.concatenate([gathered[:, :half], gathered[:, half:]], 0)


def body(value_half, out_half, saved, first_grad, head_grad):
    sections = lax.axis_size("section")
    tensors = lax.axis_size("tensor")
    copies = sections // 2
    low = tensors // 2
    position = lax.axis_index("section")
    is_lower = position < copies
    w_value, w_out = value_half[0], out_half[0]
    tok = first_grad.shape[1]

    swap_route = []
    for r in range(sections):
        for t in range(tensors):
            c, s, h, i = r // copies, r % copies, t // low, t % low
            swap_route.append((r * tensors + t, (h * copies + s) * tensors + c * low + i))
    mirror_route = [(r, (r + copies) % sections) for r in range(sections)]
    relay_route = [(r, r - 1) for r in range(1, sections)]

    def swap(block):
        return lax.ppermute(block, ("section", "tensor"), swap_route)

    def mirror(block):
        return lax.ppermute(block, "section", mirror_route)

    def both(partial):
        return partial.astype(F32) + mirror(partial).astype(F32)

    head_mine = jnp.where(is_lower, head_grad[0], head_grad[1])
    mine = jnp.concatenate([first_grad[0], saved[0, 0], saved[0, 1], head_mine], 0)
    swapped = swap(mine)
    first_swapped, head_swapped = swapped[:tok], swapped[3 * tok :]
    gathered = lax.all_gather(swapped[: 3 * tok], "tensor", axis=1, tiled=True)
    grad0 = split_copies(gathered[:tok])
    in0 = split_copies(gathered[tok : 2 * tok])
    in1 = split_copies(gathered[2 * tok :])

    def block(preact, backgrad):
        sigmoid = jax.nn.sigmoid(preact)
        act = (preact * sigmoid).astype(BF16)
        slope = sigmoid * (1.0 + preact * (1.0 - sigmoid))
        return act, (backgrad * slope).astype(BF16)

    def pass_down(pre_grad, incoming):
        partial = dot(pre_grad, w_value, 1, 1).astype(BF16)
        partial = jnp.concatenate([partial[:tok], partial[tok:]], 1)
        summed = lax.psum_scatter(partial, "tensor", scatter_dimension=1, tiled=True)
        return (incoming.astype(F32) + summed.astype(F32)).astype(BF16)

    back0 = both(dot(grad0, w_out, 1, 1).astype(BF16))
    pre0 = both(dot(in0, w_value, 1, 0).astype(BF16))
    act0, e0 = block(pre0, back0)
    pre1 = both(dot(in1, w_value, 1, 0).astype(BF16))
    passed0 = pass_down(e0, first_swapped)
    from_next = lax.ppermute(passed0, "section", relay_route)
    at_end = position % copies == copies - 1
    incoming = jnp.where(at_end, head_swapped, from_next)
    grad1 = split_copies(lax.all_gather(incoming, "tensor", axis=1, tiled=True))
    back1 = both(dot(grad1, w_out, 1, 1).astype(BF16))
    act1, e1 = block(pre1, back1)
    sent = swap(pass_down(e1, incoming))

    inputs = jnp.concatenate([in0, in1], 0)
    grads = jnp.concatenate([grad0, grad1], 0)
    value_grad = dot(inputs, jnp.concatenate([e0, e1], 0), 0, 0).astype(BF16)
    out_grad = dot(jnp.concatenate([act0, act1], 0), grads, 0, 0).astype(BF16)
    return sent[None], value_grad[None], out_grad[None]


def solution(mesh):
    return jax.shard_map(
        body,
        mesh=mesh,
        in_specs=(
            P("section", None, "tensor"),
            P("section", "tensor", None),
            P("section", None, None, "tensor"),
            P("section", None, "tensor"),
            P(None, None, "tensor"),
        ),
        out_specs=(
            P("section", None, "tensor"),
            P("section", None, "tensor"),
            P("section", "tensor", None),
        ),
        check_vma=False,
    )
```

```python
import functools

import jax
import jax.numpy as jnp
from jax import lax
from jax.experimental import pallas as pl
from jax.experimental.pallas import tpu as pltpu
from jax.sharding import PartitionSpec as P

F32 = jnp.float32
BF16 = jnp.bfloat16
MESH = pl.DeviceIdType.MESH
X0, X1, G0, G1 = 0, 1, 2, 3
P0, Q0, P1, Q1 = 0, 1, 2, 3


def dot(left, right, left_dim, right_dim):
    return lax.dot_general(
        left, right, (((left_dim,), (right_dim,)), ((), ())), preferred_element_type=F32
    )


def tiled(width, tile, step):
    tile = min(tile, width)

    @pl.loop(0, width // tile)
    def _(j):
        step(pl.ds(pl.multiple_of(j * tile, tile), tile))


def chain(
    sections, tensors,
    value_hbm, out_hbm, saved, first, head,
    xg_out, act_out, pre_out, passed_out,
    wv, wo, inb, ob, rb, act, pre, part, rs, rel,
    w_sem, loc_sem, fin_sem,
    own_s, own_r, swp_s, swp_r, oth_s, oth_r, x_s, x_r, rs_s, rs_r, g1_s, g1_r, hd_s, hd_r,
):
    copies, low = sections // 2, tensors // 2
    position, t = lax.axis_index("section"), lax.axis_index("tensor")
    side, s = position // copies, lax.rem(position, copies)
    h, i = t // low, lax.rem(t, low)
    tok, chunk = first.shape
    inner = wv.shape[1]
    rows = tok // 2
    home = h == side
    away = jnp.logical_not(home)
    at_end = s == copies - 1
    mirror = (lax.rem(position + copies, sections), t)
    swap_to = (h * copies + s, side * low + i)
    mine_rel = jnp.where(home, 0, 1)

    def peer(d):
        return (position, lax.rem(t + d, tensors))

    def cols(k):
        return pl.ds(pl.multiple_of(k * chunk, chunk), chunk)

    def remote(src, dst, send, recv, device):
        return pltpu.make_async_remote_copy(
            src_ref=src, dst_ref=dst, send_sem=send, recv_sem=recv,
            device_id=device, device_id_type=MESH,
        )

    def arrived(dst, recv):
        remote(dst, dst, own_s.at[0, 0], recv, mirror).wait_recv()

    pending = []

    def send(copy, when=None):
        if when is None:
            copy().start()
        else:
            @pl.when(when)
            def _():
                copy().start()
        pending.append((copy, when))

    load_v = pltpu.make_async_copy(value_hbm, wv, w_sem.at[0])
    load_o = pltpu.make_async_copy(out_hbm, wo, w_sem.at[1])
    load_v.start()
    load_o.start()

    barrier = pltpu.get_barrier_semaphore()

    def greet(device):
        pl.semaphore_signal(barrier, inc=1, device_id=device, device_id_type=MESH)

    greet(mirror)
    for d in range(1, tensors):
        greet(peer(d))

    @pl.when(away)
    def _():
        greet(swap_to)

    @pl.when(s > 0)
    def _():
        for u in range(tensors):
            greet((position - 1, u))

    @pl.when(s < copies - 1)
    def _():
        for u in range(tensors):
            greet((position + 1, u))

    greeted = tensors + jnp.where(away, 1, 0)
    greeted += jnp.where(s > 0, tensors, 0) + jnp.where(s < copies - 1, tensors, 0)
    pl.semaphore_wait(barrier, greeted)

    source = {X0: saved.at[0], X1: saved.at[1], G0: first}
    order = (X0, G0, X1)

    for k in order:
        for way, target in ((0, mirror), (1, swap_to)):
            part_rows = pl.ds(way * rows, rows)
            send(lambda k=k, way=way, target=target, part_rows=part_rows: remote(
                source[k].at[part_rows, :], inb.at[k, 1, part_rows, cols(i)],
                swp_s.at[k, way], swp_r.at[k], target), away)
    for k in order:
        for d in range(1, tensors):
            send(lambda k=k, d=d: remote(
                source[k], inb.at[k, 0, :, cols(i)],
                own_s.at[k, d - 1], own_r.at[k, i], peer(d)), home)

        @pl.when(home)
        def _(k=k):
            pltpu.make_async_copy(source[k], inb.at[k, 0, :, cols(i)], loc_sem.at[k]).start()

    def head_copy(d, rel_slot):
        which = side if rel_slot == 0 else 1 - side
        return remote(
            head.at[which], inb.at[G1, rel_slot, :, cols(i)],
            hd_s.at[rel_slot, d - 1], hd_r.at[rel_slot, i], peer(d))

    head_home = jnp.logical_and(home, at_end)

    def own_block(k):
        for j in range(low):
            u = side * low + j

            @pl.when(u == t)
            def _():
                pltpu.make_async_copy(source[k], inb.at[k, 0, :, cols(j)], loc_sem.at[k]).wait()

            @pl.when(u != t)
            def _():
                arrived(inb.at[k, 0, :, cols(j)], own_r.at[k, j])

    def project(kind, k, slot):
        def step(c):
            if kind in (P0, P1):
                value = dot(inb[k, slot], wv[:, c], 1, 0)
            else:
                value = dot(inb[k, slot], wo[c, :], 1, 1)
            ob[kind, slot, :, c] = value.astype(BF16)

        tiled(inner, 512, step)

    def exchange(kind, slot):
        send(lambda: remote(
            ob.at[kind, slot], rb.at[kind, 1 - slot],
            x_s.at[kind, slot], x_r.at[kind, 1 - slot], mirror))

    own_block(X0)
    load_v.wait()
    project(P0, X0, 0)
    exchange(P0, 0)
    own_block(G0)
    load_o.wait()
    project(Q0, G0, 0)
    exchange(Q0, 0)

    row_mine = pl.ds(pl.multiple_of(mine_rel * rows, rows), rows)
    for k in order:
        arrived(inb.at[k, 1, row_mine, cols(i)], swp_r.at[k])
        for d in range(1, tensors):
            send(lambda k=k, d=d: remote(
                inb.at[k, 1, row_mine, cols(i)], inb.at[k, 1, row_mine, cols(i)],
                oth_s.at[k, d - 1], oth_r.at[k, d - 1], peer(d)))

    def other_block(k):
        for d in range(1, tensors):
            u = lax.rem(t + tensors - d, tensors)
            r = pl.multiple_of(jnp.where(u // low == side, 0, rows), rows)
            arrived(inb.at[k, 1, pl.ds(r, rows), cols(lax.rem(u, low))], oth_r.at[k, d - 1])

    other_block(X0)
    project(P0, X0, 1)
    exchange(P0, 1)
    other_block(G0)
    project(Q0, G0, 1)
    exchange(Q0, 1)
    own_block(X1)
    project(P1, X1, 0)
    other_block(X1)
    project(P1, X1, 1)

    for rel_slot in range(2):
        for d in range(1, tensors):
            send(functools.partial(head_copy, d, rel_slot), head_home)

        @pl.when(head_home)
        def _(rel_slot=rel_slot):
            which = side if rel_slot == 0 else 1 - side
            pltpu.make_async_copy(
                head.at[which], inb.at[G1, rel_slot, :, cols(i)], loc_sem.at[3 + rel_slot]).start()

    def unit(tick, slot):
        p_kind, q_kind = (P0, Q0) if tick == 0 else (P1, Q1)
        arrived(rb.at[p_kind, slot], x_r.at[p_kind, slot])
        arrived(rb.at[q_kind, slot], x_r.at[q_kind, slot])

        def bend(c):
            p = ob[p_kind, slot, :, c].astype(F32) + rb[p_kind, slot, :, c].astype(F32)
            q = ob[q_kind, slot, :, c].astype(F32) + rb[q_kind, slot, :, c].astype(F32)
            sigmoid = jax.nn.sigmoid(p)
            act[tick, slot, :, c] = (p * sigmoid).astype(BF16)
            pre[tick, slot, :, c] = (q * (sigmoid * (1.0 + p * (1.0 - sigmoid)))).astype(BF16)

        tiled(inner, 256, bend)

        def back(c):
            part[tick, slot, :, c] = dot(pre[tick, slot], wv[c, :], 1, 1).astype(BF16)

        tiled(wv.shape[0], 256, back)
        for j in range(low):
            u = (side if slot == 0 else 1 - side) * low + j
            d = lax.rem(t - u + tensors, tensors)
            lane = jnp.maximum(d - 1, 0)
            send(lambda u=u, lane=lane, j=j: remote(
                part.at[tick, slot, :, cols(j)], rs.at[tick, lane],
                rs_s.at[tick, slot, j], rs_r.at[tick, lane], (position, u)), d != 0)

    def reduce(tick, incoming):
        total = part[tick, mine_rel, :, cols(i)].astype(F32)
        for d in range(1, tensors):
            arrived(rs.at[tick, d - 1], rs_r.at[tick, d - 1])
            total += rs[tick, d - 1].astype(F32)
        rel[tick] = (inb[incoming, mine_rel, :, cols(i)].astype(F32) + total).astype(BF16)

    unit(0, 1)
    exchange(P1, 0)
    unit(0, 0)
    exchange(P1, 1)
    reduce(0, G0)
    for u in range(tensors):
        send(lambda u=u: remote(
            rel.at[0], inb.at[G1, mine_rel, :, cols(i)],
            g1_s.at[u], g1_r.at[t], (position - 1, u)), s > 0)

    @pl.when(at_end)
    def _():
        for rel_slot in range(2):
            for j in range(low):
                u = side * low + j

                @pl.when(u == t)
                def _():
                    which = side if rel_slot == 0 else 1 - side
                    pltpu.make_async_copy(
                        head.at[which], inb.at[G1, rel_slot, :, cols(j)],
                        loc_sem.at[3 + rel_slot]).wait()

                @pl.when(u != t)
                def _():
                    arrived(inb.at[G1, rel_slot, :, cols(j)], hd_r.at[rel_slot, j])

    @pl.when(jnp.logical_not(at_end))
    def _():
        for u in range(tensors):
            r = jnp.where(u // low == side, 0, 1)
            arrived(inb.at[G1, r, :, cols(u % low)], g1_r.at[u])

    for slot in range(2):
        project(Q1, G1, slot)
        exchange(Q1, slot)
    xg_copy = pltpu.make_async_copy(inb, xg_out, fin_sem.at[0])
    xg_copy.start()
    unit(1, 1)
    unit(1, 0)
    act_copy = pltpu.make_async_copy(act, act_out, fin_sem.at[1])
    pre_copy = pltpu.make_async_copy(pre, pre_out, fin_sem.at[2])
    act_copy.start()
    pre_copy.start()
    reduce(1, G1)
    passed_copy = pltpu.make_async_copy(rel.at[1], passed_out, fin_sem.at[3])
    passed_copy.start()
    for copy, when in pending:
        if when is None:
            copy().wait_send()
        else:
            @pl.when(when)
            def _():
                copy().wait_send()
    for copy in (xg_copy, act_copy, pre_copy, passed_copy):
        copy.wait()


def body(value_half, out_half, saved, first_grad, head_grad):
    sections, tensors = lax.axis_size("section"), lax.axis_size("tensor")
    copies, low = sections // 2, tensors // 2
    half, inner = value_half.shape[1:]
    tok, chunk = first_grad.shape[1:]
    dma = pltpu.SemaphoreType.DMA
    hbm, vmem = pl.BlockSpec(memory_space=pl.ANY), pl.BlockSpec(memory_space=pltpu.VMEM)
    shape = jax.ShapeDtypeStruct
    xg, act, pre, passed = pl.pallas_call(
        functools.partial(chain, sections, tensors),
        out_shape=(
            shape((4, 2, tok, half), BF16),
            shape((2, 2, tok, inner), BF16),
            shape((2, 2, tok, inner), BF16),
            shape((tok, chunk), BF16),
        ),
        in_specs=[hbm, hbm, vmem, vmem, vmem],
        out_specs=(hbm, hbm, hbm, hbm),
        scratch_shapes=[
            pltpu.VMEM((half, inner), BF16),
            pltpu.VMEM((inner, half), BF16),
            pltpu.VMEM((4, 2, tok, half), BF16),
            pltpu.VMEM((4, 2, tok, inner), BF16),
            pltpu.VMEM((4, 2, tok, inner), BF16),
            pltpu.VMEM((2, 2, tok, inner), BF16),
            pltpu.VMEM((2, 2, tok, inner), BF16),
            pltpu.VMEM((2, 2, tok, half), BF16),
            pltpu.VMEM((2, tensors - 1, tok, chunk), BF16),
            pltpu.VMEM((2, tok, chunk), BF16),
            dma((2,)), dma((5,)), dma((4,)),
            dma((3, tensors - 1)), dma((3, low)),
            dma((3, 2)), dma((3,)),
            dma((3, tensors - 1)), dma((3, tensors - 1)),
            dma((4, 2)), dma((4, 2)),
            dma((2, 2, low)), dma((2, tensors - 1)),
            dma((tensors,)), dma((tensors,)),
            dma((2, tensors - 1)), dma((2, low)),
        ],
        compiler_params=pltpu.CompilerParams(
            collective_id=0, has_side_effects=True, vmem_limit_bytes=48 * 2**20
        ),
        cost_estimate=pl.CostEstimate(
            flops=24 * tok * half * inner, bytes_accessed=8 * half * inner, transcendentals=4 * tok * inner
        ),
    )(value_half[0], out_half[0], saved[0], first_grad[0], head_grad)

    swap_route = []
    for r in range(sections):
        for t in range(tensors):
            c, s, h, i = r // copies, r % copies, t // low, t % low
            swap_route.append((r * tensors + t, (h * copies + s) * tensors + c * low + i))
    sent = lax.ppermute(passed, ("section", "tensor"), swap_route)
    inputs = xg[:2].reshape(4 * tok, half)
    grads = xg[2:].reshape(4 * tok, half)
    value_grad = dot(inputs, pre.reshape(4 * tok, inner), 0, 0).astype(BF16)
    out_grad = dot(act.reshape(4 * tok, inner), grads, 0, 0).astype(BF16)
    return sent[None], value_grad[None], out_grad[None]


def solution(mesh):
    return jax.shard_map(
        body,
        mesh=mesh,
        in_specs=(
            P("section", None, "tensor"),
            P("section", "tensor", None),
            P("section", None, None, "tensor"),
            P("section", None, "tensor"),
            P(None, None, "tensor"),
        ),
        out_specs=(
            P("section", None, "tensor"),
            P("section", None, "tensor"),
            P("section", "tensor", None),
        ),
        check_vma=False,
    )
```

```python
import functools

import jax
import jax.numpy as jnp
from jax import lax
from jax.experimental import pallas as pl
from jax.experimental.pallas import tpu as pltpu
from jax.sharding import PartitionSpec as P

F32 = jnp.float32
BF16 = jnp.bfloat16
MESH = pl.DeviceIdType.MESH
X0, X1, G0, G1 = 0, 1, 2, 3
P0, Q0, P1, Q1 = 0, 1, 2, 3


def dot(left, right, left_dim, right_dim):
    return lax.dot_general(
        left, right, (((left_dim,), (right_dim,)), ((), ())), preferred_element_type=F32
    )


def tiled(width, tile, step):
    tile = min(tile, width)

    @pl.loop(0, width // tile)
    def _(j):
        step(pl.ds(pl.multiple_of(j * tile, tile), tile))


def chain(
    sections, tensors,
    value_hbm, out_hbm, saved, first, head,
    xg_out, act_out, pre_out, value_out, wide_out, passed_out,
    wv, wo, vg, og, inb, ob, rb, act, pre, part, rs, rel,
    w_sem, loc_sem, fin_sem,
    own_s, own_r, swp_s, swp_r, oth_s, oth_r, x_s, x_r, rs_s, rs_r, g1_s, g1_r, hd_s, hd_r,
):
    copies, low = sections // 2, tensors // 2
    position, t = lax.axis_index("section"), lax.axis_index("tensor")
    side, s = position // copies, lax.rem(position, copies)
    h, i = t // low, lax.rem(t, low)
    tok, chunk = first.shape
    inner = wv.shape[1]
    rows = tok // 2
    home = h == side
    away = jnp.logical_not(home)
    at_end = s == copies - 1
    mirror = (lax.rem(position + copies, sections), t)
    swap_to = (h * copies + s, side * low + i)
    mine_rel = jnp.where(home, 0, 1)

    def peer(d):
        return (position, lax.rem(t + d, tensors))

    def cols(k):
        return pl.ds(pl.multiple_of(k * chunk, chunk), chunk)

    def remote(src, dst, send, recv, device):
        return pltpu.make_async_remote_copy(
            src_ref=src, dst_ref=dst, send_sem=send, recv_sem=recv,
            device_id=device, device_id_type=MESH,
        )

    def arrived(dst, recv):
        remote(dst, dst, own_s.at[0, 0], recv, mirror).wait_recv()

    pending = []

    def send(copy, when=None):
        if when is None:
            copy().start()
        else:
            @pl.when(when)
            def _():
                copy().start()
        pending.append((copy, when))

    load_v = pltpu.make_async_copy(value_hbm, wv, w_sem.at[0])
    load_o = pltpu.make_async_copy(out_hbm, wo, w_sem.at[1])
    load_v.start()
    load_o.start()

    barrier = pltpu.get_barrier_semaphore()

    def greet(device):
        pl.semaphore_signal(barrier, inc=1, device_id=device, device_id_type=MESH)

    greet(mirror)
    for d in range(1, tensors):
        greet(peer(d))

    @pl.when(away)
    def _():
        greet(swap_to)

    @pl.when(s > 0)
    def _():
        for u in range(tensors):
            greet((position - 1, u))

    @pl.when(s < copies - 1)
    def _():
        for u in range(tensors):
            greet((position + 1, u))

    greeted = tensors + jnp.where(away, 1, 0)
    greeted += jnp.where(s > 0, tensors, 0) + jnp.where(s < copies - 1, tensors, 0)
    pl.semaphore_wait(barrier, greeted)

    source = {X0: saved.at[0], X1: saved.at[1], G0: first}
    order = (X0, G0, X1)

    for k in order:
        for way, target in ((0, mirror), (1, swap_to)):
            part_rows = pl.ds(way * rows, rows)
            send(lambda k=k, way=way, target=target, part_rows=part_rows: remote(
                source[k].at[part_rows, :], inb.at[k, 1, part_rows, cols(i)],
                swp_s.at[k, way], swp_r.at[k], target), away)
    for k in order:
        for d in range(1, tensors):
            send(lambda k=k, d=d: remote(
                source[k], inb.at[k, 0, :, cols(i)],
                own_s.at[k, d - 1], own_r.at[k, i], peer(d)), home)

        @pl.when(home)
        def _(k=k):
            pltpu.make_async_copy(source[k], inb.at[k, 0, :, cols(i)], loc_sem.at[k]).start()

    def head_copy(d, rel_slot):
        which = side if rel_slot == 0 else 1 - side
        return remote(
            head.at[which], inb.at[G1, rel_slot, :, cols(i)],
            hd_s.at[rel_slot, d - 1], hd_r.at[rel_slot, i], peer(d))

    head_home = jnp.logical_and(home, at_end)

    def own_block(k):
        for j in range(low):
            u = side * low + j

            @pl.when(u == t)
            def _():
                pltpu.make_async_copy(source[k], inb.at[k, 0, :, cols(j)], loc_sem.at[k]).wait()

            @pl.when(u != t)
            def _():
                arrived(inb.at[k, 0, :, cols(j)], own_r.at[k, j])

    def project(kind, k, slot):
        def step(c):
            if kind in (P0, P1):
                value = dot(inb[k, slot], wv[:, c], 1, 0)
            else:
                value = dot(inb[k, slot], wo[c, :], 1, 1)
            ob[kind, slot, :, c] = value.astype(BF16)

        tiled(inner, 512, step)

    def product(kind, slot):
        return remote(
            ob.at[kind, slot], rb.at[kind, 1 - slot],
            x_s.at[kind, slot], x_r.at[kind, 1 - slot], mirror)

    def exchange(kind, slot):
        send(functools.partial(product, kind, slot))

    own_block(X0)
    load_v.wait()
    project(P0, X0, 0)
    exchange(P0, 0)
    own_block(G0)
    load_o.wait()
    project(Q0, G0, 0)
    exchange(Q0, 0)

    row_mine = pl.ds(pl.multiple_of(mine_rel * rows, rows), rows)
    for k in order:
        arrived(inb.at[k, 1, row_mine, cols(i)], swp_r.at[k])
        for d in range(1, tensors):
            send(lambda k=k, d=d: remote(
                inb.at[k, 1, row_mine, cols(i)], inb.at[k, 1, row_mine, cols(i)],
                oth_s.at[k, d - 1], oth_r.at[k, d - 1], peer(d)))

    def other_block(k):
        for d in range(1, tensors):
            u = lax.rem(t + tensors - d, tensors)
            r = pl.multiple_of(jnp.where(u // low == side, 0, rows), rows)
            arrived(inb.at[k, 1, pl.ds(r, rows), cols(lax.rem(u, low))], oth_r.at[k, d - 1])

    other_block(X0)
    project(P0, X0, 1)
    exchange(P0, 1)
    other_block(G0)
    project(Q0, G0, 1)
    exchange(Q0, 1)
    own_block(X1)
    project(P1, X1, 0)
    exchange(P1, 0)
    other_block(X1)
    project(P1, X1, 1)

    for rel_slot in range(2):
        for d in range(1, tensors):
            send(functools.partial(head_copy, d, rel_slot), head_home)

        @pl.when(head_home)
        def _(rel_slot=rel_slot):
            which = side if rel_slot == 0 else 1 - side
            pltpu.make_async_copy(
                head.at[which], inb.at[G1, rel_slot, :, cols(i)], loc_sem.at[3 + rel_slot]).start()

    def unit(tick, slot, on_arrival=lambda: None):
        p_kind, q_kind = (P0, Q0) if tick == 0 else (P1, Q1)
        arrived(rb.at[p_kind, slot], x_r.at[p_kind, slot])
        arrived(rb.at[q_kind, slot], x_r.at[q_kind, slot])
        on_arrival()

        def bend(c):
            p = ob[p_kind, slot, :, c].astype(F32) + rb[p_kind, slot, :, c].astype(F32)
            q = ob[q_kind, slot, :, c].astype(F32) + rb[q_kind, slot, :, c].astype(F32)
            sigmoid = jax.nn.sigmoid(p)
            act[tick, slot, :, c] = (p * sigmoid).astype(BF16)
            pre[tick, slot, :, c] = (q * (sigmoid * (1.0 + p * (1.0 - sigmoid)))).astype(BF16)

        tiled(inner, 256, bend)

        def back(c):
            part[tick, slot, :, c] = dot(pre[tick, slot], wv[c, :], 1, 1).astype(BF16)

        tiled(wv.shape[0], 256, back)
        for j in range(low):
            u = (side if slot == 0 else 1 - side) * low + j
            d = lax.rem(t - u + tensors, tensors)
            lane = jnp.maximum(d - 1, 0)
            send(lambda u=u, lane=lane, j=j: remote(
                part.at[tick, slot, :, cols(j)], rs.at[tick, lane],
                rs_s.at[tick, slot, j], rs_r.at[tick, lane], (position, u)), d != 0)

    def reduce(tick, incoming):
        total = part[tick, mine_rel, :, cols(i)].astype(F32)
        for d in range(1, tensors):
            arrived(rs.at[tick, d - 1], rs_r.at[tick, d - 1])
            total += rs[tick, d - 1].astype(F32)
        rel[tick] = (inb[incoming, mine_rel, :, cols(i)].astype(F32) + total).astype(BF16)

    unit(0, 1, lambda: exchange(P1, 1))
    unit(0, 0)
    reduce(0, G0)
    for u in range(tensors):
        send(lambda u=u: remote(
            rel.at[0], inb.at[G1, mine_rel, :, cols(i)],
            g1_s.at[u], g1_r.at[t], (position - 1, u)), s > 0)

    @pl.when(at_end)
    def _():
        for rel_slot in range(2):
            for j in range(low):
                u = side * low + j

                @pl.when(u == t)
                def _():
                    which = side if rel_slot == 0 else 1 - side
                    pltpu.make_async_copy(
                        head.at[which], inb.at[G1, rel_slot, :, cols(j)],
                        loc_sem.at[3 + rel_slot]).wait()

                @pl.when(u != t)
                def _():
                    arrived(inb.at[G1, rel_slot, :, cols(j)], hd_r.at[rel_slot, j])

    @pl.when(jnp.logical_not(at_end))
    def _():
        for u in range(tensors):
            r = jnp.where(u // low == side, 0, 1)
            arrived(inb.at[G1, r, :, cols(u % low)], g1_r.at[u])

    local = []

    def store(src, dst):
        copy = pltpu.make_async_copy(src, dst, fin_sem.at[len(local)])
        copy.start()
        local.append(copy)

    def flat(ref):
        return ref.reshape(2 * tok, ref.shape[-1])

    project(Q1, G1, 0)
    product(Q1, 0).start()
    project(Q1, G1, 1)
    store(inb.at[X1], xg_out.at[0])
    store(inb.at[G1], xg_out.at[1])

    def value_term(c):
        vg[:, c] = dot(flat(inb[X0]), flat(pre[0, :, :, c]), 0, 0).astype(BF16)

    def wide_term(c):
        og[c, :] = dot(flat(act[0, :, :, c]), flat(inb[G0]), 0, 0).astype(BF16)

    tiled(inner, 256, value_term)
    store(vg, value_out)
    tiled(inner, 256, wide_term)
    store(og, wide_out)
    product(Q1, 0).wait_send()
    exchange(Q1, 1)
    for slot in (1, 0):
        unit(1, slot)
        store(act.at[1, slot], act_out.at[slot])
        store(pre.at[1, slot], pre_out.at[slot])
    reduce(1, G1)
    store(rel.at[1], passed_out)
    for copy, when in pending:
        if when is None:
            copy().wait_send()
        else:
            @pl.when(when)
            def _():
                copy().wait_send()
    for copy in local:
        copy.wait()


def body(value_half, out_half, saved, first_grad, head_grad):
    sections, tensors = lax.axis_size("section"), lax.axis_size("tensor")
    copies, low = sections // 2, tensors // 2
    half, inner = value_half.shape[1:]
    tok, chunk = first_grad.shape[1:]
    dma = pltpu.SemaphoreType.DMA
    hbm = pl.BlockSpec(memory_space=pl.ANY)
    shape = jax.ShapeDtypeStruct
    xg, act, pre, value0, wide0, passed = pl.pallas_call(
        functools.partial(chain, sections, tensors),
        out_shape=(
            shape((2, 2, tok, half), BF16),
            shape((2, tok, inner), BF16),
            shape((2, tok, inner), BF16),
            shape((half, inner), BF16),
            shape((inner, half), BF16),
            shape((tok, chunk), BF16),
        ),
        in_specs=[hbm] * 5,
        out_specs=(hbm,) * 6,
        scratch_shapes=[
            pltpu.VMEM((half, inner), BF16),
            pltpu.VMEM((inner, half), BF16),
            pltpu.VMEM((half, inner), BF16),
            pltpu.VMEM((inner, half), BF16),
            pltpu.VMEM((4, 2, tok, half), BF16),
            pltpu.VMEM((4, 2, tok, inner), BF16),
            pltpu.VMEM((4, 2, tok, inner), BF16),
            pltpu.VMEM((2, 2, tok, inner), BF16),
            pltpu.VMEM((2, 2, tok, inner), BF16),
            pltpu.VMEM((2, 2, tok, half), BF16),
            pltpu.VMEM((2, tensors - 1, tok, chunk), BF16),
            pltpu.VMEM((2, tok, chunk), BF16),
            dma((2,)), dma((5,)), dma((9,)),
            dma((3, tensors - 1)), dma((3, low)),
            dma((3, 2)), dma((3,)),
            dma((3, tensors - 1)), dma((3, tensors - 1)),
            dma((4, 2)), dma((4, 2)),
            dma((2, 2, low)), dma((2, tensors - 1)),
            dma((tensors,)), dma((tensors,)),
            dma((2, tensors - 1)), dma((2, low)),
        ],
        compiler_params=pltpu.CompilerParams(
            collective_id=0, has_side_effects=True, vmem_limit_bytes=48 * 2**20
        ),
        cost_estimate=pl.CostEstimate(
            flops=24 * tok * half * inner, bytes_accessed=8 * half * inner, transcendentals=4 * tok * inner
        ),
    )(value_half[0], out_half[0], saved[0], first_grad[0], head_grad)

    swap_route = []
    for r in range(sections):
        for t in range(tensors):
            c, s, h, i = r // copies, r % copies, t // low, t % low
            swap_route.append((r * tensors + t, (h * copies + s) * tensors + c * low + i))
    sent = lax.ppermute(passed, ("section", "tensor"), swap_route)
    inputs, grads = xg[0].reshape(2 * tok, half), xg[1].reshape(2 * tok, half)
    value1 = dot(inputs, pre.reshape(2 * tok, inner), 0, 0)
    wide1 = dot(act.reshape(2 * tok, inner), grads, 0, 0)
    value_grad = (value0.astype(F32) + value1).astype(BF16)
    out_grad = (wide0.astype(F32) + wide1).astype(BF16)
    return sent[None], value_grad[None], out_grad[None]


def solution(mesh):
    return jax.shard_map(
        body,
        mesh=mesh,
        in_specs=(
            P("section", None, "tensor"),
            P("section", "tensor", None),
            P("section", None, None, "tensor"),
            P("section", None, "tensor"),
            P(None, None, "tensor"),
        ),
        out_specs=(
            P("section", None, "tensor"),
            P("section", None, "tensor"),
            P("section", "tensor", None),
        ),
        check_vma=False,
    )
```

```python
import functools

import jax
import jax.numpy as jnp
from jax import lax
from jax.experimental import pallas as pl
from jax.experimental.pallas import tpu as pltpu
from jax.sharding import PartitionSpec as P

F32 = jnp.float32
BF16 = jnp.bfloat16
MESH = pl.DeviceIdType.MESH
X0, X1, G0, G1 = 0, 1, 2, 3
P0, Q0, P1, Q1 = 0, 1, 2, 3


def dot(left, right, left_dim, right_dim):
    return lax.dot_general(
        left, right, (((left_dim,), (right_dim,)), ((), ())), preferred_element_type=F32
    )


def tiled(width, tile, step):
    tile = min(tile, width)

    @pl.loop(0, width // tile)
    def _(j):
        step(pl.ds(pl.multiple_of(j * tile, tile), tile))


def chain(
    sections, tensors,
    value_hbm, out_hbm, saved, first, head,
    xg_out, act_out, pre_out, value_out, wide_out, passed_out,
    wv, wo, vg, og, inb, via, ob, rb, act, pre, part, rs, rel,
    w_sem, loc_sem, fin_sem,
    own_s, own_r, swp_s, swp_r, via_s, via_r, oth_s, oth_r, x_s, x_r, rs_s, rs_r, g1_s, g1_r, hd_s, hd_r,
):
    copies, low = sections // 2, tensors // 2
    position, t = lax.axis_index("section"), lax.axis_index("tensor")
    side, s = position // copies, lax.rem(position, copies)
    h, i = t // low, lax.rem(t, low)
    tok, chunk = first.shape
    inner = wv.shape[1]
    rows = tok // 2
    home = h == side
    away = jnp.logical_not(home)
    at_end = s == copies - 1
    mirror = (lax.rem(position + copies, sections), t)
    home_peer = (position, side * low + i)
    mine_rel = jnp.where(home, 0, 1)

    def peer(d):
        return (position, lax.rem(t + d, tensors))

    def cols(k):
        return pl.ds(pl.multiple_of(k * chunk, chunk), chunk)

    def remote(src, dst, send, recv, device):
        return pltpu.make_async_remote_copy(
            src_ref=src, dst_ref=dst, send_sem=send, recv_sem=recv,
            device_id=device, device_id_type=MESH,
        )

    def arrived(dst, recv):
        remote(dst, dst, own_s.at[0, 0], recv, mirror).wait_recv()

    pending = []

    def send(copy, when=None):
        if when is None:
            copy().start()
        else:
            @pl.when(when)
            def _():
                copy().start()
        pending.append((copy, when))

    load_v = pltpu.make_async_copy(value_hbm, wv, w_sem.at[0])
    load_o = pltpu.make_async_copy(out_hbm, wo, w_sem.at[1])
    load_v.start()
    load_o.start()

    barrier = pltpu.get_barrier_semaphore()

    def greet(device):
        pl.semaphore_signal(barrier, inc=1, device_id=device, device_id_type=MESH)

    greet(mirror)
    for d in range(1, tensors):
        greet(peer(d))

    @pl.when(s > 0)
    def _():
        for u in range(tensors):
            greet((position - 1, u))

    @pl.when(s < copies - 1)
    def _():
        for u in range(tensors):
            greet((position + 1, u))

    greeted = tensors + jnp.where(s > 0, tensors, 0) + jnp.where(s < copies - 1, tensors, 0)
    pl.semaphore_wait(barrier, greeted)

    source = {X0: saved.at[0], X1: saved.at[1], G0: first}
    order = (X0, G0, X1)

    def rows_of(way):
        return pl.ds(way * rows, rows)

    for k in order:
        send(lambda k=k: remote(
            source[k].at[rows_of(0), :], inb.at[k, 1, rows_of(0), cols(i)],
            swp_s.at[k], swp_r.at[k], mirror), away)
        send(lambda k=k: remote(
            source[k].at[rows_of(1), :], via.at[k],
            via_s.at[k], via_r.at[k], home_peer), away)
    for k in order:
        for d in range(1, tensors):
            send(lambda k=k, d=d: remote(
                source[k], inb.at[k, 0, :, cols(i)],
                own_s.at[k, d - 1], own_r.at[k, i], peer(d)), home)

        @pl.when(home)
        def _(k=k):
            pltpu.make_async_copy(source[k], inb.at[k, 0, :, cols(i)], loc_sem.at[k]).start()

    for k in order:
        @pl.when(home)
        def _(k=k):
            arrived(via.at[k], via_r.at[k])

        send(lambda k=k: remote(
            via.at[k], inb.at[k, 1, rows_of(1), cols(i)],
            swp_s.at[k], swp_r.at[k], mirror), home)

    def head_copy(d, rel_slot):
        which = side if rel_slot == 0 else 1 - side
        return remote(
            head.at[which], inb.at[G1, rel_slot, :, cols(i)],
            hd_s.at[rel_slot, d - 1], hd_r.at[rel_slot, i], peer(d))

    head_home = jnp.logical_and(home, at_end)

    def own_block(k):
        for j in range(low):
            u = side * low + j

            @pl.when(u == t)
            def _():
                pltpu.make_async_copy(source[k], inb.at[k, 0, :, cols(j)], loc_sem.at[k]).wait()

            @pl.when(u != t)
            def _():
                arrived(inb.at[k, 0, :, cols(j)], own_r.at[k, j])

    def project(kind, k, slot):
        def step(c):
            if kind in (P0, P1):
                value = dot(inb[k, slot], wv[:, c], 1, 0)
            else:
                value = dot(inb[k, slot], wo[c, :], 1, 1)
            ob[kind, slot, :, c] = value.astype(BF16)

        tiled(inner, 512, step)

    def product(kind, slot):
        return remote(
            ob.at[kind, slot], rb.at[kind, 1 - slot],
            x_s.at[kind, slot], x_r.at[kind, 1 - slot], mirror)

    def exchange(kind, slot):
        send(functools.partial(product, kind, slot))

    own_block(X0)
    load_v.wait()
    project(P0, X0, 0)
    exchange(P0, 0)
    own_block(G0)
    load_o.wait()
    project(Q0, G0, 0)
    exchange(Q0, 0)

    row_mine = pl.ds(pl.multiple_of(mine_rel * rows, rows), rows)
    for k in order:
        arrived(inb.at[k, 1, row_mine, cols(i)], swp_r.at[k])
        for d in range(1, tensors):
            send(lambda k=k, d=d: remote(
                inb.at[k, 1, row_mine, cols(i)], inb.at[k, 1, row_mine, cols(i)],
                oth_s.at[k, d - 1], oth_r.at[k, d - 1], peer(d)))

    def other_block(k):
        for d in range(1, tensors):
            u = lax.rem(t + tensors - d, tensors)
            r = pl.multiple_of(jnp.where(u // low == side, 0, rows), rows)
            arrived(inb.at[k, 1, pl.ds(r, rows), cols(lax.rem(u, low))], oth_r.at[k, d - 1])

    other_block(X0)
    project(P0, X0, 1)
    exchange(P0, 1)
    other_block(G0)
    project(Q0, G0, 1)
    exchange(Q0, 1)
    own_block(X1)
    project(P1, X1, 0)
    exchange(P1, 0)
    other_block(X1)
    project(P1, X1, 1)

    for rel_slot in range(2):
        for d in range(1, tensors):
            send(functools.partial(head_copy, d, rel_slot), head_home)

        @pl.when(head_home)
        def _(rel_slot=rel_slot):
            which = side if rel_slot == 0 else 1 - side
            pltpu.make_async_copy(
                head.at[which], inb.at[G1, rel_slot, :, cols(i)], loc_sem.at[3 + rel_slot]).start()

    def unit(tick, slot, on_arrival=lambda: None):
        p_kind, q_kind = (P0, Q0) if tick == 0 else (P1, Q1)
        arrived(rb.at[p_kind, slot], x_r.at[p_kind, slot])
        arrived(rb.at[q_kind, slot], x_r.at[q_kind, slot])
        on_arrival()

        def bend(c):
            p = ob[p_kind, slot, :, c].astype(F32) + rb[p_kind, slot, :, c].astype(F32)
            q = ob[q_kind, slot, :, c].astype(F32) + rb[q_kind, slot, :, c].astype(F32)
            sigmoid = jax.nn.sigmoid(p)
            act[tick, slot, :, c] = (p * sigmoid).astype(BF16)
            pre[tick, slot, :, c] = (q * (sigmoid * (1.0 + p * (1.0 - sigmoid)))).astype(BF16)

        tiled(inner, 256, bend)

        def back(c):
            part[tick, slot, :, c] = dot(pre[tick, slot], wv[c, :], 1, 1).astype(BF16)

        tiled(wv.shape[0], 256, back)
        for j in range(low):
            u = (side if slot == 0 else 1 - side) * low + j
            d = lax.rem(t - u + tensors, tensors)
            lane = jnp.maximum(d - 1, 0)
            send(lambda u=u, lane=lane, j=j: remote(
                part.at[tick, slot, :, cols(j)], rs.at[tick, lane],
                rs_s.at[tick, slot, j], rs_r.at[tick, lane], (position, u)), d != 0)

    def reduce(tick, incoming):
        total = part[tick, mine_rel, :, cols(i)].astype(F32)
        for d in range(1, tensors):
            arrived(rs.at[tick, d - 1], rs_r.at[tick, d - 1])
            total += rs[tick, d - 1].astype(F32)
        rel[tick] = (inb[incoming, mine_rel, :, cols(i)].astype(F32) + total).astype(BF16)

    unit(0, 1, lambda: exchange(P1, 1))
    unit(0, 0)
    reduce(0, G0)
    for u in range(tensors):
        send(lambda u=u: remote(
            rel.at[0], inb.at[G1, mine_rel, :, cols(i)],
            g1_s.at[u], g1_r.at[t], (position - 1, u)), s > 0)

    @pl.when(at_end)
    def _():
        for rel_slot in range(2):
            for j in range(low):
                u = side * low + j

                @pl.when(u == t)
                def _():
                    which = side if rel_slot == 0 else 1 - side
                    pltpu.make_async_copy(
                        head.at[which], inb.at[G1, rel_slot, :, cols(j)],
                        loc_sem.at[3 + rel_slot]).wait()

                @pl.when(u != t)
                def _():
                    arrived(inb.at[G1, rel_slot, :, cols(j)], hd_r.at[rel_slot, j])

    @pl.when(jnp.logical_not(at_end))
    def _():
        for u in range(tensors):
            r = jnp.where(u // low == side, 0, 1)
            arrived(inb.at[G1, r, :, cols(u % low)], g1_r.at[u])

    local = []

    def store(src, dst):
        copy = pltpu.make_async_copy(src, dst, fin_sem.at[len(local)])
        copy.start()
        local.append(copy)

    def flat(ref):
        return ref.reshape(2 * tok, ref.shape[-1])

    project(Q1, G1, 0)
    product(Q1, 0).start()
    project(Q1, G1, 1)
    store(inb.at[X1], xg_out.at[0])
    store(inb.at[G1], xg_out.at[1])

    def value_term(c):
        vg[:, c] = dot(flat(inb[X0]), flat(pre[0, :, :, c]), 0, 0).astype(BF16)

    def wide_term(c):
        og[c, :] = dot(flat(act[0, :, :, c]), flat(inb[G0]), 0, 0).astype(BF16)

    tiled(inner, 256, value_term)
    store(vg, value_out)
    tiled(inner, 256, wide_term)
    store(og, wide_out)
    product(Q1, 0).wait_send()
    exchange(Q1, 1)
    for slot in (1, 0):
        unit(1, slot)
        store(act.at[1, slot], act_out.at[slot])
        store(pre.at[1, slot], pre_out.at[slot])
    reduce(1, G1)
    store(rel.at[1], passed_out)
    for copy, when in pending:
        if when is None:
            copy().wait_send()
        else:
            @pl.when(when)
            def _():
                copy().wait_send()
    for copy in local:
        copy.wait()


def body(value_half, out_half, saved, first_grad, head_grad):
    sections, tensors = lax.axis_size("section"), lax.axis_size("tensor")
    copies, low = sections // 2, tensors // 2
    half, inner = value_half.shape[1:]
    tok, chunk = first_grad.shape[1:]
    dma = pltpu.SemaphoreType.DMA
    hbm = pl.BlockSpec(memory_space=pl.ANY)
    shape = jax.ShapeDtypeStruct
    xg, act, pre, value0, wide0, passed = pl.pallas_call(
        functools.partial(chain, sections, tensors),
        out_shape=(
            shape((2, 2, tok, half), BF16),
            shape((2, tok, inner), BF16),
            shape((2, tok, inner), BF16),
            shape((half, inner), BF16),
            shape((inner, half), BF16),
            shape((tok, chunk), BF16),
        ),
        in_specs=[hbm] * 5,
        out_specs=(hbm,) * 6,
        scratch_shapes=[
            pltpu.VMEM((half, inner), BF16),
            pltpu.VMEM((inner, half), BF16),
            pltpu.VMEM((half, inner), BF16),
            pltpu.VMEM((inner, half), BF16),
            pltpu.VMEM((4, 2, tok, half), BF16),
            pltpu.VMEM((3, tok // 2, chunk), BF16),
            pltpu.VMEM((4, 2, tok, inner), BF16),
            pltpu.VMEM((4, 2, tok, inner), BF16),
            pltpu.VMEM((2, 2, tok, inner), BF16),
            pltpu.VMEM((2, 2, tok, inner), BF16),
            pltpu.VMEM((2, 2, tok, half), BF16),
            pltpu.VMEM((2, tensors - 1, tok, chunk), BF16),
            pltpu.VMEM((2, tok, chunk), BF16),
            dma((2,)), dma((5,)), dma((9,)),
            dma((3, tensors - 1)), dma((3, low)),
            dma((3,)), dma((3,)), dma((3,)), dma((3,)),
            dma((3, tensors - 1)), dma((3, tensors - 1)),
            dma((4, 2)), dma((4, 2)),
            dma((2, 2, low)), dma((2, tensors - 1)),
            dma((tensors,)), dma((tensors,)),
            dma((2, tensors - 1)), dma((2, low)),
        ],
        compiler_params=pltpu.CompilerParams(
            collective_id=0, has_side_effects=True, vmem_limit_bytes=62 * 2**20
        ),
        cost_estimate=pl.CostEstimate(
            flops=24 * tok * half * inner, bytes_accessed=8 * half * inner, transcendentals=4 * tok * inner
        ),
    )(value_half[0], out_half[0], saved[0], first_grad[0], head_grad)

    swap_route = []
    for r in range(sections):
        for t in range(tensors):
            c, s, h, i = r // copies, r % copies, t // low, t % low
            swap_route.append((r * tensors + t, (h * copies + s) * tensors + c * low + i))
    sent = lax.ppermute(passed, ("section", "tensor"), swap_route)
    inputs, grads = xg[0].reshape(2 * tok, half), xg[1].reshape(2 * tok, half)
    value1 = dot(inputs, pre.reshape(2 * tok, inner), 0, 0)
    wide1 = dot(act.reshape(2 * tok, inner), grads, 0, 0)
    value_grad = (value0.astype(F32) + value1).astype(BF16)
    out_grad = (wide0.astype(F32) + wide1).astype(BF16)
    return sent[None], value_grad[None], out_grad[None]


def solution(mesh):
    return jax.shard_map(
        body,
        mesh=mesh,
        in_specs=(
            P("section", None, "tensor"),
            P("section", "tensor", None),
            P("section", None, None, "tensor"),
            P("section", None, "tensor"),
            P(None, None, "tensor"),
        ),
        out_specs=(
            P("section", None, "tensor"),
            P("section", None, "tensor"),
            P("section", "tensor", None),
        ),
        check_vma=False,
    )
```
